32 devices in a mesh: ctx: 8 (over y, x, core), tp: 4 (over z).
Axes of the slice: x: 2, y: 2, z: 4, core: 2. Of those that a mesh axis runs over, the one named last changes fastest.
Arguments:
- hidden: bfloat16 [2048, 8192], P('ctx', 'tp'), may hold values from -6 to 6
- w_feature: bfloat16 [8192, 3, 8192], P('ctx', None, 'tp'), may hold values from -0.0625 to 0.0625
- short_filter: float32 [7, 3, 8192], P(None, None, 'tp'), may hold values from -2.4 to 2.4
- mr_filter: bfloat16 [512, 128], P('tp'), may hold values from -0.5 to 0.5
- w_out: bfloat16 [8192, 8192], P('tp'), may hold values from -0.09375 to 0.09375
Outputs:
- mixed: bfloat16 [2048, 8192], P('ctx', 'tp')
The draws below stay inside these ranges and needn't reach their ends.
All inputs are finite; a program needn't handle non-finite values.
Results may differ from the reference program's by a relative error of at most 0.024.
Values may be sent and summed in bfloat16 or wider, within the bound.
A program may use at most 128 MiB of HBM per device.

```python
import jax
import jax.numpy as jnp
from jax import lax

D = 8192
TAPS_SHORT = 7
TAPS_MR = 128
GROUP = 16
SEQ = 2048
N_CTX = 8


def spiked(entries, key, source, target, shards_of, factor):
    owner, partner = [(jnp.arange(entries.shape[position]) // (entries.shape[position] // shards_of)).reshape([-1 if axis == position else 1 for axis in range(entries.ndim)]) for position in (source, target)]
    chosen = jax.random.permutation(key, shards_of)[partner]
    strong = (owner == chosen) | (owner == (partner + shards_of // 2) % shards_of)
    return jnp.where(strong, factor * entries, entries)


def level_of(stream_key, extent, pieces, least, high):
    loudness = 1.0
    for axis_at, blocks in pieces:
        steps = jax.random.uniform(jax.random.fold_in(jax.random.fold_in(stream_key, 6), axis_at), (blocks,), jnp.float32, least / len(pieces), high / len(pieces))
        loudness = loudness * jnp.repeat(jnp.exp(steps), extent[axis_at] // blocks).reshape((-1,) + (1,) * (len(extent) - 1 - axis_at))
    return loudness


def gaussian(stream_key, shape, deviation, most, pieces=(), kind=jnp.bfloat16):
    level = level_of(stream_key, shape, pieces, -0.22, 0.18) if pieces else 1.0
    array = jax.random.normal(stream_key, shape, jnp.float32) * deviation * level
    return jnp.minimum(jnp.maximum(array, -most), most).astype(kind)


def bell_draw_with(own_key, dims, scale, most, split, heavy, held_as=jnp.bfloat16):
    array = scale * jax.random.normal(own_key, dims, jnp.float32)
    if split:
        array = array * level_of(own_key, dims, split, -0.22, 0.18)
    return jnp.clip(spiked(array, jax.random.fold_in(own_key, 3), *heavy), -most, most).astype(held_as)


def setup_inputs(seed: int = 0) -> dict:
    key_list = jax.random.split(jax.random.key(seed), 6)
    hidden = bell_draw_with(key_list[0], (SEQ, D), 1.0, 6.0, ((0, 8), (1, 4)), (1, 0, 8, 2.0))
    w_feature = gaussian(key_list[1], (D, 3, D), D ** -0.5, 0.0625, ((0, 8), (2, 4)))
    short_filter = gaussian(key_list[2], (TAPS_SHORT, 3, D), 0.4, 2.4, ((2, 4),), jnp.float32)
    mr_filter = gaussian(key_list[3], (D // GROUP, TAPS_MR), TAPS_MR ** -0.5, 0.5, ((0, 4),))
    w_out = bell_draw_with(key_list[4], (D, D), D ** -0.5, 0.09375, ((0, 4),), (0, 1, 4, 2.0))
    return dict(hidden=hidden, w_feature=w_feature, short_filter=short_filter, mr_filter=mr_filter, w_out=w_out)


def short_filtering(padded, tap_weights, row_count):
    running = jnp.zeros((row_count,) + padded.shape[1:], jnp.float32)
    for shift_by in range(TAPS_SHORT):
        row_start = TAPS_SHORT - 1 - shift_by
        running = running + tap_weights[shift_by] * padded[row_start:row_start + row_count]
    return running


def reference(hidden, w_feature, short_filter, mr_filter, w_out):
    feature_block = D // N_CTX
    flat_weight = w_feature.reshape(D, 3 * D)

    def add_block(running, block_index):
        row_start = block_index * feature_block
        columns = lax.dynamic_slice_in_dim(hidden, row_start, feature_block, 1)
        weights = lax.dynamic_slice_in_dim(flat_weight, row_start, feature_block, 0)
        partial_sum = jnp.dot(columns, weights, preferred_element_type=jnp.float32).astype(jnp.bfloat16)
        partial_sum = lax.optimization_barrier(partial_sum)
        return running + partial_sum.astype(jnp.float32), None

    projected, unused = lax.scan(add_block, jnp.zeros((SEQ, 3 * D), jnp.float32),
                                 jnp.arange(N_CTX, dtype=jnp.int32))
    projected = projected.reshape(SEQ, 3, D)
    padded = jnp.pad(projected, ((TAPS_SHORT - 1, 0), (0, 0), (0, 0)))
    streams = short_filtering(padded, short_filter, SEQ)
    gated_rows = (streams[:, 1] * streams[:, 2]).astype(jnp.bfloat16)
    gated_rows = lax.optimization_barrier(gated_rows)
    channel_taps = jnp.repeat(mr_filter.astype(jnp.float32), GROUP, axis=0)
    gated_pad = jnp.pad(gated_rows.astype(jnp.float32), ((TAPS_MR - 1, 0), (0, 0)))

    def add_tap(running, tap_index):
        shifted = lax.dynamic_slice_in_dim(gated_pad, TAPS_MR - 1 - tap_index, SEQ, 0)
        weight_row = lax.dynamic_slice_in_dim(channel_taps, tap_index, 1, 1)[:, 0]
        return running + shifted * weight_row[None, :], None

    long_out, unused_taps = lax.scan(add_tap, jnp.zeros((SEQ, D), jnp.float32),
                                     jnp.arange(TAPS_MR, dtype=jnp.int32))
    mixer_rows = (streams[:, 0] * long_out).astype(jnp.bfloat16)
    return jnp.dot(mixer_rows, w_out, preferred_element_type=jnp.float32).astype(jnp.bfloat16)
```

```python
import functools

import jax
import jax.numpy as jnp
from jax import lax
from jax.experimental import pallas as pl
from jax.experimental.pallas import tpu as pltpu
from jax.sharding import PartitionSpec as P

TAPS_SHORT = 7
TAPS_MR = 128
GROUP = 16
LANES = 128
RIM = 16
VMEM_LIMIT = 48 * 1024 * 1024


def params():
    return pltpu.CompilerParams(vmem_limit_bytes=VMEM_LIMIT)


def passed_along(value, axis, by):
    count = lax.axis_size(axis)
    pairs = [(i, i + by) for i in range(count) if 0 <= i + by < count]
    return lax.ppermute(value, axis, pairs)


def toeplitz_kernel(row_ref, out_ref):
    for g in range(row_ref.shape[0]):
        row = jnp.broadcast_to(row_ref[g : g + 1, :], out_ref.shape[1:])
        out_ref[g] = pltpu.roll(row, 0, 1, stride=1, stride_axis=0).astype(out_ref.dtype)


def toeplitz_of(filters):
    groups = filters.shape[0]
    per = LANES // GROUP
    rows = jnp.pad(filters[:, ::-1].astype(jnp.float32), ((0, 0), (1, TAPS_MR - 1)))
    return pl.pallas_call(
        toeplitz_kernel,
        grid=(groups // per,),
        in_specs=[pl.BlockSpec((per, 2 * TAPS_MR), lambda i: (i, 0))],
        out_specs=pl.BlockSpec((per, TAPS_MR, 2 * TAPS_MR), lambda i: (i, 0, 0)),
        out_shape=jax.ShapeDtypeStruct((groups, TAPS_MR, 2 * TAPS_MR), jnp.bfloat16),
        compiler_params=params(),
        name="toeplitz",
    )(rows)


def short_filtering(rim, value, taps):
    rows = value.shape[0]
    ext = jnp.concatenate([rim.astype(jnp.float32), value.astype(jnp.float32)], 0)
    running = jnp.zeros(value.shape, jnp.float32)
    for shift_by in range(TAPS_SHORT):
        start = rim.shape[0] - shift_by
        running = running + taps[shift_by : shift_by + 1] * ext[start : start + rows]
    return running


def gate_kernel(k_ref, v_ref, kr_ref, vr_ref, kt_ref, vt_ref, out_ref):
    k = short_filtering(kr_ref[...], k_ref[...], kt_ref[...])
    v = short_filtering(vr_ref[...], v_ref[...], vt_ref[...])
    out_ref[...] = (k * v).astype(out_ref.dtype)


def gating(k, v, k_rim, v_rim, k_taps, v_taps):
    rows, width = k.shape
    tile = min(width, 256)
    whole = pl.BlockSpec((rows, tile), lambda i: (0, i))
    rim = pl.BlockSpec((k_rim.shape[0], tile), lambda i: (0, i))
    taps = pl.BlockSpec((TAPS_SHORT, tile), lambda i: (0, i))
    return pl.pallas_call(
        gate_kernel,
        grid=(width // tile,),
        in_specs=[whole, whole, rim, rim, taps, taps],
        out_specs=whole,
        out_shape=jax.ShapeDtypeStruct(k.shape, jnp.bfloat16),
        compiler_params=params(),
        name="gate",
    )(k, v, k_rim, v_rim, k_taps, v_taps)


def long_kernel(g_ref, r_ref, t_ref, out_ref):
    per = t_ref.shape[0]
    ext = jnp.concatenate([r_ref[...], g_ref[...]], 0)
    blocks = g_ref.shape[0] // TAPS_MR
    windows = jnp.concatenate(
        [ext[b * TAPS_MR : (b + 2) * TAPS_MR] for b in range(blocks)], 1
    )
    matrix = t_ref[...].reshape(per * TAPS_MR, 2 * TAPS_MR)
    result = jnp.dot(matrix, windows, preferred_element_type=jnp.float32)
    lane = lax.broadcasted_iota(jnp.int32, (TAPS_MR, blocks * LANES), 1) % LANES // GROUP
    chosen = result[:TAPS_MR]
    for g in range(1, per):
        chosen = jnp.where(lane == g, result[g * TAPS_MR : (g + 1) * TAPS_MR], chosen)
    for b in range(blocks):
        out_ref[b * TAPS_MR : (b + 1) * TAPS_MR] = chosen[:, b * LANES : (b + 1) * LANES]


def long_filtering(gated, rim, toeplitz):
    rows, width = gated.shape
    per = LANES // GROUP
    spec = pl.BlockSpec((rows, LANES), lambda i: (0, i))
    return pl.pallas_call(
        long_kernel,
        grid=(width // LANES,),
        in_specs=[
            spec,
            pl.BlockSpec((TAPS_MR, LANES), lambda i: (0, i)),
            pl.BlockSpec((per, TAPS_MR, 2 * TAPS_MR), lambda i: (i, 0, 0)),
        ],
        out_specs=spec,
        out_shape=jax.ShapeDtypeStruct(gated.shape, jnp.float32),
        compiler_params=params(),
        cost_estimate=pl.CostEstimate(
            flops=4 * rows * width * per * TAPS_MR,
            bytes_accessed=toeplitz.size * 2 + rows * width * 8,
            transcendentals=0,
        ),
        name="long",
    )(gated, rim, toeplitz)


def out_kernel(q_ref, qr_ref, qt_ref, l_ref, w_ref, out_ref, mixer_ref):
    @pl.when(pl.program_id(0) == 0)
    def _():
        width = q_ref.shape[1]
        tile = min(width, 256)
        for at in range(0, width, tile):
            cols = slice(at, at + tile)
            q = short_filtering(qr_ref[:, cols], q_ref[:, cols], qt_ref[:, cols])
            mixer_ref[:, cols] = (q * l_ref[:, cols]).astype(mixer_ref.dtype)

    out_ref[0] = jnp.dot(
        mixer_ref[...], w_ref[...], preferred_element_type=jnp.float32
    ).astype(out_ref.dtype)


def out_projection(q, q_rim, q_taps, long_out, w_out, slabs):
    rows, width = q.shape
    slab = w_out.shape[1] // slabs
    tile = min(slab, 512)
    per = slab // tile
    whole = lambda a: pl.BlockSpec(a.shape, lambda i: (0, 0))
    return pl.pallas_call(
        out_kernel,
        grid=(slabs * per,),
        in_specs=[
            whole(q), whole(q_rim), whole(q_taps), whole(long_out),
            pl.BlockSpec((width, tile), lambda i: (0, i)),
        ],
        out_specs=pl.BlockSpec((1, rows, tile), lambda i: (i // per, 0, i % per)),
        out_shape=jax.ShapeDtypeStruct((slabs, rows, slab), jnp.bfloat16),
        scratch_shapes=[pltpu.VMEM((rows, width), jnp.bfloat16)],
        compiler_params=params(),
        name="out",
    )(q, q_rim, q_taps, long_out, w_out)


def local(hidden, w_feature, short_filter, mr_filter, w_out):
    rows = hidden.shape[0]
    feature_block = w_feature.shape[0]
    n_tp = lax.axis_size("tp")
    n_ctx = lax.axis_size("ctx")
    parts = hidden.shape[1] // feature_block
    blocked = jnp.swapaxes(hidden.reshape(rows, parts, feature_block), 0, 1)
    gathered = lax.all_gather(blocked, "tp", axis=0, tiled=True)
    toeplitz = toeplitz_of(mr_filter)
    gathered, toeplitz = lax.optimization_barrier((gathered, toeplitz))
    columns = lax.all_to_all(gathered, "ctx", split_axis=0, concat_axis=0, tiled=True)
    columns = columns.reshape(n_ctx * rows, feature_block)

    def stream(p, operand):
        partial_sum = jnp.dot(
            operand, w_feature[:, p], preferred_element_type=jnp.float32
        ).astype(jnp.bfloat16)
        return partial_sum

    def scattered(partial_sum):
        return lax.psum_scatter(partial_sum, "ctx", scatter_dimension=0, tiled=True)

    k = scattered(stream(1, columns))
    v = scattered(stream(2, columns))
    q = scattered(stream(0, columns))
    k_rim = passed_along(k[rows - RIM :], "ctx", 1)
    v_rim = passed_along(v[rows - RIM :], "ctx", 1)
    gated = gating(k, v, k_rim, v_rim, short_filter[:, 1], short_filter[:, 2])
    gated_rim = passed_along(gated[rows - TAPS_MR :], "ctx", 1)
    long_out = long_filtering(gated, gated_rim, toeplitz)
    q_rim = passed_along(q[rows - RIM :], "ctx", 1)
    partial_out = out_projection(q, q_rim, short_filter[:, 0], long_out, w_out, n_tp)
    summed = lax.psum_scatter(partial_out, "tp", scatter_dimension=0, tiled=True)
    return summed.reshape(rows, -1)


def solution(mesh):
    return jax.shard_map(
        local,
        mesh=mesh,
        in_specs=(
            P("ctx", "tp"),
            P("ctx", None, "tp"),
            P(None, None, "tp"),
            P("tp", None),
            P("tp", None),
        ),
        out_specs=P("ctx", "tp"),
        check_vma=False,
    )
```

```python
import functools

import jax
import jax.numpy as jnp
from jax import lax
from jax.experimental import pallas as pl
from jax.experimental.pallas import tpu as pltpu
from jax.sharding import PartitionSpec as P

TAPS_SHORT = 7
TAPS_MR = 128
GROUP = 16
LANES = 128
RIM = 16
VMEM_LIMIT = 48 * 1024 * 1024


def params():
    return pltpu.CompilerParams(vmem_limit_bytes=VMEM_LIMIT)


def passed_along(value, axis, by):
    count = lax.axis_size(axis)
    pairs = [(i, i + by) for i in range(count) if 0 <= i + by < count]
    return lax.ppermute(value, axis, pairs)


def toeplitz_kernel(row_ref, out_ref):
    for g in range(row_ref.shape[0]):
        row = jnp.broadcast_to(row_ref[g : g + 1, :], out_ref.shape[1:])
        out_ref[g] = pltpu.roll(row, 0, 1, stride=1, stride_axis=0).astype(out_ref.dtype)


def toeplitz_of(filters):
    groups = filters.shape[0]
    per = LANES // GROUP
    rows = jnp.pad(filters[:, ::-1].astype(jnp.float32), ((0, 0), (1, TAPS_MR - 1)))
    return pl.pallas_call(
        toeplitz_kernel,
        grid=(groups // per,),
        in_specs=[pl.BlockSpec((per, 2 * TAPS_MR), lambda i: (i, 0))],
        out_specs=pl.BlockSpec((per, TAPS_MR, 2 * TAPS_MR), lambda i: (i, 0, 0)),
        out_shape=jax.ShapeDtypeStruct((groups, TAPS_MR, 2 * TAPS_MR), jnp.bfloat16),
        compiler_params=params(),
        name="toeplitz",
    )(rows)


def short_filtering(rim, value, taps):
    rows = value.shape[0]
    ext = jnp.concatenate([rim.astype(jnp.float32), value.astype(jnp.float32)], 0)
    running = jnp.zeros(value.shape, jnp.float32)
    for shift_by in range(TAPS_SHORT):
        start = rim.shape[0] - shift_by
        running = running + taps[shift_by : shift_by + 1] * ext[start : start + rows]
    return running


def gate_kernel(k_ref, v_ref, kr_ref, vr_ref, kt_ref, vt_ref, out_ref):
    k = short_filtering(kr_ref[...], k_ref[...], kt_ref[...])
    v = short_filtering(vr_ref[...], v_ref[...], vt_ref[...])
    out_ref[...] = (k * v).astype(out_ref.dtype)


def gating(k, v, k_rim, v_rim, k_taps, v_taps):
    rows, width = k.shape
    tile = min(width, 256)
    whole = pl.BlockSpec((rows, tile), lambda i: (0, i))
    rim = pl.BlockSpec((k_rim.shape[0], tile), lambda i: (0, i))
    taps = pl.BlockSpec((TAPS_SHORT, tile), lambda i: (0, i))
    return pl.pallas_call(
        gate_kernel,
        grid=(width // tile,),
        in_specs=[whole, whole, rim, rim, taps, taps],
        out_specs=whole,
        out_shape=jax.ShapeDtypeStruct(k.shape, jnp.bfloat16),
        compiler_params=params(),
        name="gate",
    )(k, v, k_rim, v_rim, k_taps, v_taps)


def long_kernel(g_ref, r_ref, t_ref, out_ref):
    per = t_ref.shape[0]
    ext = jnp.concatenate([r_ref[...], g_ref[...]], 0)
    blocks = g_ref.shape[0] // TAPS_MR
    windows = jnp.concatenate(
        [ext[b * TAPS_MR : (b + 2) * TAPS_MR] for b in range(blocks)], 1
    )
    matrix = t_ref[...].reshape(per * TAPS_MR, 2 * TAPS_MR)
    result = jnp.dot(matrix, windows, preferred_element_type=jnp.float32)
    lane = lax.broadcasted_iota(jnp.int32, (TAPS_MR, blocks * LANES), 1) % LANES // GROUP
    chosen = result[:TAPS_MR]
    for g in range(1, per):
        chosen = jnp.where(lane == g, result[g * TAPS_MR : (g + 1) * TAPS_MR], chosen)
    for b in range(blocks):
        out_ref[b * TAPS_MR : (b + 1) * TAPS_MR] = chosen[:, b * LANES : (b + 1) * LANES]


def long_filtering(gated, rim, toeplitz):
    rows, width = gated.shape
    per = LANES // GROUP
    spec = pl.BlockSpec((rows, LANES), lambda i: (0, i))
    return pl.pallas_call(
        long_kernel,
        grid=(width // LANES,),
        in_specs=[
            spec,
            pl.BlockSpec((TAPS_MR, LANES), lambda i: (0, i)),
            pl.BlockSpec((per, TAPS_MR, 2 * TAPS_MR), lambda i: (i, 0, 0)),
        ],
        out_specs=spec,
        out_shape=jax.ShapeDtypeStruct(gated.shape, jnp.float32),
        compiler_params=params(),
        cost_estimate=pl.CostEstimate(
            flops=4 * rows * width * per * TAPS_MR,
            bytes_accessed=toeplitz.size * 2 + rows * width * 8,
            transcendentals=0,
        ),
        name="long",
    )(gated, rim, toeplitz)


def out_kernel(q_ref, qr_ref, qt_ref, l_ref, w_ref, out_ref, mixer_ref):
    @pl.when(pl.program_id(0) == 0)
    def _():
        width = q_ref.shape[1]
        tile = min(width, 256)
        for at in range(0, width, tile):
            cols = slice(at, at + tile)
            q = short_filtering(qr_ref[:, cols], q_ref[:, cols], qt_ref[:, cols])
            mixer_ref[:, cols] = (q * l_ref[:, cols]).astype(mixer_ref.dtype)

    out_ref[0] = jnp.dot(
        mixer_ref[...], w_ref[...], preferred_element_type=jnp.float32
    ).astype(out_ref.dtype)


def out_projection(q, q_rim, q_taps, long_out, w_out, slabs):
    rows, width = q.shape
    slab = w_out.shape[1] // slabs
    tile = min(slab, 512)
    per = slab // tile
    whole = lambda a: pl.BlockSpec(a.shape, lambda i: (0, 0))
    return pl.pallas_call(
        out_kernel,
        grid=(slabs * per,),
        in_specs=[
            whole(q), whole(q_rim), whole(q_taps), whole(long_out),
            pl.BlockSpec((width, tile), lambda i: (0, i)),
        ],
        out_specs=pl.BlockSpec((1, rows, tile), lambda i: (i // per, 0, i % per)),
        out_shape=jax.ShapeDtypeStruct((slabs, rows, slab), jnp.bfloat16),
        scratch_shapes=[pltpu.VMEM((rows, width), jnp.bfloat16)],
        compiler_params=params(),
        name="out",
    )(q, q_rim, q_taps, long_out, w_out)


def flipped(index, bit):
    value = 1 << bit
    return index + value - 2 * value * (index // value % 2)


def feature_kernel(n, bits, tiles, x_ref, w_ref, out_ref, *scratch):
    own, held, sent, got = (
        scratch[0], scratch[1:bits], scratch[bits : 2 * bits], scratch[2 * bits : 3 * bits]
    )
    send_sem, recv_sem = scratch[3 * bits :]
    step = pl.program_id(0)
    me = lax.axis_index("ctx")
    rows = x_ref.shape[0] // n
    half = w_ref.shape[2] // 2
    orders = (list(range(1, bits)), list(range(2, bits)) + [1])

    def copy_of(stage, sub, chunk):
        bit = 0 if stage == 0 else orders[sub][stage - 1]
        slot = chunk % 2
        return pltpu.make_async_remote_copy(
            src_ref=sent[stage].at[slot, sub],
            dst_ref=got[stage].at[chunk, sub],
            send_sem=send_sem.at[stage, sub, slot],
            recv_sem=recv_sem.at[stage, sub, chunk],
            device_id={"ctx": flipped(me, bit)},
            device_id_type=pl.DeviceIdType.MESH,
        )

    @pl.when(step == 0)
    def _():
        barrier = pltpu.get_barrier_semaphore()
        for bit in range(bits):
            pl.semaphore_signal(
                barrier, inc=1, device_id={"ctx": flipped(me, bit)},
                device_id_type=pl.DeviceIdType.MESH,
            )
        pl.semaphore_wait(barrier, bits)

    @pl.when(step < tiles)
    def _():
        slot = step % 2
        for mine in (0, 1):
            target_ref = own if mine else sent[0]
            for m in range(n // 2):
                r = 2 * m + 1 - mine
                target = me
                for bit in range(bits):
                    if r >> bit & 1:
                        target = flipped(target, bit)
                block = x_ref[pl.ds(pl.multiple_of(target * rows, rows), rows), :]
                product = jnp.dot(
                    block, w_ref[0], preferred_element_type=jnp.float32
                ).astype(jnp.bfloat16)
                for sub in (0, 1):
                    place = 0
                    for bit in orders[sub]:
                        place = 2 * place + (r >> bit & 1)
                    target_ref[slot, sub, place * rows : (place + 1) * rows] = product[
                        :, sub * half : (sub + 1) * half
                    ]
            if not mine:
                for sub in (0, 1):
                    copy_of(0, sub, step).start()

    for stage in range(1, bits + 1):
        chunk = step - stage

        @pl.when(jnp.logical_and(chunk >= 0, chunk < tiles))
        def _():
            slot = chunk % 2
            before = own if stage == 1 else held[stage - 2]
            keep = rows * (n >> (stage + 1))
            for sub in (0, 1):
                copy_of(stage - 1, sub, chunk).wait()
                for part in ((1, 0) if stage < bits else (0,)):
                    size = keep if stage < bits else rows
                    at = slice(part * size, (part + 1) * size)
                    total = before[slot, sub, at].astype(jnp.float32) + got[stage - 1][
                        chunk, sub, at
                    ].astype(jnp.float32)
                    if stage == bits:
                        out_ref[0, :, sub * half : (sub + 1) * half] = total.astype(out_ref.dtype)
                    elif part:
                        sent[stage][slot, sub] = total.astype(jnp.bfloat16)
                        copy_of(stage, sub, chunk).start()
                    else:
                        held[stage - 1][slot, sub] = total


def featurizer(x, w, n):
    bits = n.bit_length() - 1
    assert n == 1 << bits and bits >= 2
    rows = x.shape[0] // n
    streams, depth, width = w.shape
    tile = min(width, 512)
    half = tile // 2
    per = width // tile
    tiles = streams * per

    def into(i):
        i = jnp.minimum(i, tiles - 1)
        return i // per, 0, i % per

    def outof(i):
        i = jnp.maximum(i - bits, 0)
        return i // per, 0, i % per

    def buffer(slots, blocks, dtype):
        return pltpu.VMEM((slots, 2, blocks * rows, half), dtype)

    return pl.pallas_call(
        functools.partial(feature_kernel, n, bits, tiles),
        grid=(tiles + bits,),
        in_specs=[
            pl.BlockSpec(x.shape, lambda i: (0, 0)),
            pl.BlockSpec((1, depth, tile), into),
        ],
        out_specs=pl.BlockSpec((1, rows, tile), outof),
        out_shape=jax.ShapeDtypeStruct((streams, rows, width), jnp.bfloat16),
        scratch_shapes=[buffer(2, n // 2, jnp.bfloat16)]
        + [buffer(2, n >> (s + 1), jnp.float32) for s in range(1, bits)]
        + [buffer(2, n >> (s + 1), jnp.bfloat16) for s in range(bits)]
        + [buffer(tiles, n >> (s + 1), jnp.bfloat16) for s in range(bits)]
        + [
            pltpu.SemaphoreType.DMA((bits, 2, 2)),
            pltpu.SemaphoreType.DMA((bits, 2, tiles)),
        ],
        compiler_params=pltpu.CompilerParams(
            vmem_limit_bytes=56 * 1024 * 1024, collective_id=0, has_side_effects=True
        ),
        cost_estimate=pl.CostEstimate(
            flops=2 * x.shape[0] * depth * width * streams,
            bytes_accessed=2 * w.size,
            transcendentals=0,
        ),
        name="featurizer",
    )(x, w)


def local(hidden, w_feature, short_filter, mr_filter, w_out):
    rows = hidden.shape[0]
    feature_block = w_feature.shape[0]
    n_tp = lax.axis_size("tp")
    n_ctx = lax.axis_size("ctx")
    parts = hidden.shape[1] // feature_block
    blocked = jnp.swapaxes(hidden.reshape(rows, parts, feature_block), 0, 1)
    gathered = lax.all_gather(blocked, "tp", axis=0, tiled=True)
    toeplitz = toeplitz_of(mr_filter)
    gathered, toeplitz = lax.optimization_barrier((gathered, toeplitz))
    columns = lax.all_to_all(gathered, "ctx", split_axis=0, concat_axis=0, tiled=True)
    columns = columns.reshape(n_ctx * rows, feature_block)

    q, k, v = featurizer(columns, jnp.swapaxes(w_feature, 0, 1), n_ctx)
    q_rim, k_rim, v_rim = passed_along(
        jnp.stack([q[rows - RIM :], k[rows - RIM :], v[rows - RIM :]]), "ctx", 1
    )
    gated = gating(k, v, k_rim, v_rim, short_filter[:, 1], short_filter[:, 2])
    gated_rim = passed_along(gated[rows - TAPS_MR :], "ctx", 1)
    long_out = long_filtering(gated, gated_rim, toeplitz)
    partial_out = out_projection(q, q_rim, short_filter[:, 0], long_out, w_out, n_tp)
    summed = lax.psum_scatter(partial_out, "tp", scatter_dimension=0, tiled=True)
    return summed.reshape(rows, -1)


def solution(mesh):
    return jax.shard_map(
        local,
        mesh=mesh,
        in_specs=(
            P("ctx", "tp"),
            P("ctx", None, "tp"),
            P(None, None, "tp"),
            P("tp", None),
            P("tp", None),
        ),
        out_specs=P("ctx", "tp"),
        check_vma=False,
    )
```

```python
import functools

import jax
import jax.numpy as jnp
from jax import lax
from jax.experimental import pallas as pl
from jax.experimental.pallas import tpu as pltpu
from jax.sharding import PartitionSpec as P

TAPS_SHORT = 7
TAPS_MR = 128
GROUP = 16
LANES = 128
RIM = 16
VMEM_LIMIT = 48 * 1024 * 1024


def params():
    return pltpu.CompilerParams(vmem_limit_bytes=VMEM_LIMIT)


def passed_along(value, axis, by):
    count = lax.axis_size(axis)
    pairs = [(i, i + by) for i in range(count) if 0 <= i + by < count]
    return lax.ppermute(value, axis, pairs)


def toeplitz_kernel(row_ref, out_ref):
    for g in range(row_ref.shape[0]):
        row = jnp.broadcast_to(row_ref[g : g + 1, :], out_ref.shape[1:])
        out_ref[g] = pltpu.roll(row, 0, 1, stride=1, stride_axis=0).astype(out_ref.dtype)


def toeplitz_of(filters):
    groups = filters.shape[0]
    per = LANES // GROUP
    rows = jnp.pad(filters[:, ::-1].astype(jnp.float32), ((0, 0), (1, TAPS_MR - 1)))
    return pl.pallas_call(
        toeplitz_kernel,
        grid=(groups // per,),
        in_specs=[pl.BlockSpec((per, 2 * TAPS_MR), lambda i: (i, 0))],
        out_specs=pl.BlockSpec((per, TAPS_MR, 2 * TAPS_MR), lambda i: (i, 0, 0)),
        out_shape=jax.ShapeDtypeStruct((groups, TAPS_MR, 2 * TAPS_MR), jnp.bfloat16),
        compiler_params=params(),
        name="toeplitz",
    )(rows)


def short_filtering(rim, value, taps):
    rows = value.shape[0]
    ext = jnp.concatenate([rim.astype(jnp.float32), value.astype(jnp.float32)], 0)
    running = jnp.zeros(value.shape, jnp.float32)
    for shift_by in range(TAPS_SHORT):
        start = rim.shape[0] - shift_by
        running = running + taps[shift_by : shift_by + 1] * ext[start : start + rows]
    return running


def gate_kernel(k_ref, v_ref, kr_ref, vr_ref, kt_ref, vt_ref, out_ref):
    k = short_filtering(kr_ref[...], k_ref[...], kt_ref[...])
    v = short_filtering(vr_ref[...], v_ref[...], vt_ref[...])
    out_ref[...] = (k * v).astype(out_ref.dtype)


def gating(k, v, k_rim, v_rim, k_taps, v_taps):
    rows, width = k.shape
    tile = min(width, 256)
    whole = pl.BlockSpec((rows, tile), lambda i: (0, i))
    rim = pl.BlockSpec((k_rim.shape[0], tile), lambda i: (0, i))
    taps = pl.BlockSpec((TAPS_SHORT, tile), lambda i: (0, i))
    return pl.pallas_call(
        gate_kernel,
        grid=(width // tile,),
        in_specs=[whole, whole, rim, rim, taps, taps],
        out_specs=whole,
        out_shape=jax.ShapeDtypeStruct(k.shape, jnp.bfloat16),
        compiler_params=params(),
        name="gate",
    )(k, v, k_rim, v_rim, k_taps, v_taps)


def long_kernel(g_ref, r_ref, t_ref, out_ref):
    per = t_ref.shape[0]
    ext = jnp.concatenate([r_ref[...], g_ref[...]], 0)
    blocks = g_ref.shape[0] // TAPS_MR
    windows = jnp.concatenate(
        [ext[b * TAPS_MR : (b + 2) * TAPS_MR] for b in range(blocks)], 1
    )
    matrix = t_ref[...].reshape(per * TAPS_MR, 2 * TAPS_MR)
    result = jnp.dot(matrix, windows, preferred_element_type=jnp.float32)
    lane = lax.broadcasted_iota(jnp.int32, (TAPS_MR, blocks * LANES), 1) % LANES // GROUP
    chosen = result[:TAPS_MR]
    for g in range(1, per):
        chosen = jnp.where(lane == g, result[g * TAPS_MR : (g + 1) * TAPS_MR], chosen)
    for b in range(blocks):
        out_ref[b * TAPS_MR : (b + 1) * TAPS_MR] = chosen[:, b * LANES : (b + 1) * LANES]


def long_filtering(gated, rim, toeplitz):
    rows, width = gated.shape
    per = LANES // GROUP
    spec = pl.BlockSpec((rows, LANES), lambda i: (0, i))
    return pl.pallas_call(
        long_kernel,
        grid=(width // LANES,),
        in_specs=[
            spec,
            pl.BlockSpec((TAPS_MR, LANES), lambda i: (0, i)),
            pl.BlockSpec((per, TAPS_MR, 2 * TAPS_MR), lambda i: (i, 0, 0)),
        ],
        out_specs=spec,
        out_shape=jax.ShapeDtypeStruct(gated.shape, jnp.float32),
        compiler_params=params(),
        cost_estimate=pl.CostEstimate(
            flops=4 * rows * width * per * TAPS_MR,
            bytes_accessed=toeplitz.size * 2 + rows * width * 8,
            transcendentals=0,
        ),
        name="long",
    )(gated, rim, toeplitz)


def out_kernel(q_ref, qr_ref, qt_ref, l_ref, w_ref, out_ref, mixer_ref):
    @pl.when(pl.program_id(0) == 0)
    def _():
        width = q_ref.shape[1]
        tile = min(width, 256)
        for at in range(0, width, tile):
            cols = slice(at, at + tile)
            q = short_filtering(qr_ref[:, cols], q_ref[:, cols], qt_ref[:, cols])
            mixer_ref[:, cols] = (q * l_ref[:, cols]).astype(mixer_ref.dtype)

    out_ref[0] = jnp.dot(
        mixer_ref[...], w_ref[...], preferred_element_type=jnp.float32
    ).astype(out_ref.dtype)


def out_projection(q, q_rim, q_taps, long_out, w_out, slabs):
    rows, width = q.shape
    slab = w_out.shape[1] // slabs
    tile = min(slab, 1024)
    per = slab // tile
    whole = lambda a: pl.BlockSpec(a.shape, lambda i: (0, 0))
    return pl.pallas_call(
        out_kernel,
        grid=(slabs * per,),
        in_specs=[
            whole(q), whole(q_rim), whole(q_taps), whole(long_out),
            pl.BlockSpec((width, tile), lambda i: (0, i)),
        ],
        out_specs=pl.BlockSpec((1, rows, tile), lambda i: (i // per, 0, i % per)),
        out_shape=jax.ShapeDtypeStruct((slabs, rows, slab), jnp.bfloat16),
        scratch_shapes=[pltpu.VMEM((rows, width), jnp.bfloat16)],
        compiler_params=params(),
        name="out",
    )(q, q_rim, q_taps, long_out, w_out)


def flipped(index, bit):
    value = 1 << bit
    return index + value - 2 * value * (index // value % 2)


def feature_kernel(n, bits, tiles, x_ref, w_ref, out_ref, *scratch):
    own, held, sent, got = (
        scratch[0], scratch[1:bits], scratch[bits : 2 * bits], scratch[2 * bits : 3 * bits]
    )
    send_sem, recv_sem = scratch[3 * bits :]
    step = pl.program_id(0)
    me = lax.axis_index("ctx")
    rows = x_ref.shape[0] // n
    half = w_ref.shape[2] // 2
    orders = (list(range(1, bits)), list(range(2, bits)) + [1])

    def copy_of(stage, sub, chunk):
        bit = 0 if stage == 0 else orders[sub][stage - 1]
        slot = chunk % 2
        return pltpu.make_async_remote_copy(
            src_ref=sent[stage].at[slot, sub],
            dst_ref=got[stage].at[chunk, sub],
            send_sem=send_sem.at[stage, sub, slot],
            recv_sem=recv_sem.at[stage, sub, chunk],
            device_id={"ctx": flipped(me, bit)},
            device_id_type=pl.DeviceIdType.MESH,
        )

    @pl.when(step == 0)
    def _():
        barrier = pltpu.get_barrier_semaphore()
        for bit in range(bits):
            pl.semaphore_signal(
                barrier, inc=1, device_id={"ctx": flipped(me, bit)},
                device_id_type=pl.DeviceIdType.MESH,
            )
        pl.semaphore_wait(barrier, bits)

    @pl.when(step < tiles)
    def _():
        slot = step % 2
        for mine in (0, 1):
            target_ref = own if mine else sent[0]
            for m in range(n // 2):
                r = 2 * m + 1 - mine
                target = me
                for bit in range(bits):
                    if r >> bit & 1:
                        target = flipped(target, bit)
                block = x_ref[pl.ds(pl.multiple_of(target * rows, rows), rows), :]
                product = jnp.dot(
                    block, w_ref[0], preferred_element_type=jnp.float32
                ).astype(jnp.bfloat16)
                for sub in (0, 1):
                    place = 0
                    for bit in orders[sub]:
                        place = 2 * place + (r >> bit & 1)
                    target_ref[slot, sub, place * rows : (place + 1) * rows] = product[
                        :, sub * half : (sub + 1) * half
                    ]
            if not mine:
                for sub in (0, 1):
                    copy_of(0, sub, step).start()

    for stage in range(1, bits + 1):
        chunk = step - stage

        @pl.when(jnp.logical_and(chunk >= 0, chunk < tiles))
        def _():
            slot = chunk % 2
            before = own if stage == 1 else held[stage - 2]
            keep = rows * (n >> (stage + 1))
            for sub in (0, 1):
                copy_of(stage - 1, sub, chunk).wait()
                for part in ((1, 0) if stage < bits else (0,)):
                    size = keep if stage < bits else rows
                    at = slice(part * size, (part + 1) * size)
                    total = before[slot, sub, at].astype(jnp.float32) + got[stage - 1][
                        chunk, sub, at
                    ].astype(jnp.float32)
                    if stage == bits:
                        out_ref[0, :, sub * half : (sub + 1) * half] = total.astype(out_ref.dtype)
                    elif part:
                        sent[stage][slot, sub] = total.astype(jnp.bfloat16)
                        copy_of(stage, sub, chunk).start()
                    else:
                        held[stage - 1][slot, sub] = total


def featurizer(x, w, n):
    bits = n.bit_length() - 1
    assert n == 1 << bits and bits >= 2
    rows = x.shape[0] // n
    streams, depth, width = w.shape
    tile = min(width, 512)
    half = tile // 2
    per = width // tile
    tiles = streams * per

    def into(i):
        i = jnp.minimum(i, tiles - 1)
        return i // per, 0, i % per

    def outof(i):
        i = jnp.maximum(i - bits, 0)
        return i // per, 0, i % per

    def buffer(slots, blocks, dtype):
        return pltpu.VMEM((slots, 2, blocks * rows, half), dtype)

    return pl.pallas_call(
        functools.partial(feature_kernel, n, bits, tiles),
        grid=(tiles + bits,),
        in_specs=[
            pl.BlockSpec(x.shape, lambda i: (0, 0)),
            pl.BlockSpec((1, depth, tile), into),
        ],
        out_specs=pl.BlockSpec((1, rows, tile), outof),
        out_shape=jax.ShapeDtypeStruct((streams, rows, width), jnp.bfloat16),
        scratch_shapes=[buffer(2, n // 2, jnp.bfloat16)]
        + [buffer(2, n >> (s + 1), jnp.float32) for s in range(1, bits)]
        + [buffer(2, n >> (s + 1), jnp.bfloat16) for s in range(bits)]
        + [buffer(tiles, n >> (s + 1), jnp.bfloat16) for s in range(bits)]
        + [
            pltpu.SemaphoreType.DMA((bits, 2, 2)),
            pltpu.SemaphoreType.DMA((bits, 2, tiles)),
        ],
        compiler_params=pltpu.CompilerParams(
            vmem_limit_bytes=56 * 1024 * 1024, collective_id=0, has_side_effects=True
        ),
        cost_estimate=pl.CostEstimate(
            flops=2 * x.shape[0] * depth * width * streams,
            bytes_accessed=2 * w.size,
            transcendentals=0,
        ),
        name="featurizer",
    )(x, w)


def local(hidden, w_feature, short_filter, mr_filter, w_out):
    rows = hidden.shape[0]
    feature_block = w_feature.shape[0]
    n_tp = lax.axis_size("tp")
    n_ctx = lax.axis_size("ctx")
    parts = hidden.shape[1] // feature_block
    blocked = jnp.swapaxes(hidden.reshape(rows, parts, feature_block), 0, 1)
    gathered = lax.all_gather(blocked, "tp", axis=0, tiled=True)
    toeplitz = toeplitz_of(mr_filter)
    gathered, toeplitz = lax.optimization_barrier((gathered, toeplitz))
    columns = lax.all_to_all(gathered, "ctx", split_axis=0, concat_axis=0, tiled=True)
    columns = columns.reshape(n_ctx * rows, feature_block)

    q, k, v = featurizer(columns, jnp.swapaxes(w_feature, 0, 1), n_ctx)
    q_rim, k_rim, v_rim = passed_along(
        jnp.stack([q[rows - RIM :], k[rows - RIM :], v[rows - RIM :]]), "ctx", 1
    )
    gated = gating(k, v, k_rim, v_rim, short_filter[:, 1], short_filter[:, 2])
    gated_rim = passed_along(gated[rows - TAPS_MR :], "ctx", 1)
    long_out = long_filtering(gated, gated_rim, toeplitz)
    partial_out = out_projection(q, q_rim, short_filter[:, 0], long_out, w_out, n_tp)
    summed = lax.psum_scatter(partial_out, "tp", scatter_dimension=0, tiled=True)
    return summed.reshape(rows, -1)


def solution(mesh):
    return jax.shard_map(
        local,
        mesh=mesh,
        in_specs=(
            P("ctx", "tp"),
            P("ctx", None, "tp"),
            P(None, None, "tp"),
            P("tp", None),
            P("tp", None),
        ),
        out_specs=P("ctx", "tp"),
        check_vma=False,
    )
```
